32 devices in a mesh: groups: 2 (over y), row: 8 (over z, x), col: 2 (over core).
Axes of the slice: x: 2, y: 2, z: 4, core: 2. Of those that a mesh axis runs over, the one named last changes fastest.
Arguments:
- first_counts: bfloat16 [4, 16, 262144], P('groups', None, ('row', 'col')), parts along dimension 0, may hold values from 1 to 100
- depth: int32 [4, 16, 262144], P('groups', None, ('row', 'col')), parts along dimension 0, may hold values from 6 to 8
- sources: int32 [4, 16], P('groups'), parts along dimension 0, may hold values from 0 to 262143
- tile_pos: int32 [16, 2, 48], P(('groups', 'row'), 'col'), parts along dimension 0, may hold values from 0 to 16383, as said below
- tile_live: int32 [16, 2], P(('groups', 'row'), 'col'), parts along dimension 0, may hold values from 6 to 48, as said below
- tile_bits: int32 [16, 2, 48, 64, 512], P(('groups', 'row'), 'col'), parts along dimension 0, may hold values from 0 to 255, as said below
Outputs:
- dependency: float32 [4, 16, 262144], P('groups', None, ('row', 'col')), parts along dimension 0
- centrality: float32 [524288], P(('groups', 'row', 'col')), parts along dimension 0
The draws below stay inside these ranges and needn't reach their ends.
There are 2 independent parts, one for each index of `groups`. The reference program is written for one: setup_inputs(seed, part) draws one part's arguments, and reference() takes and returns one part's arrays. A program takes and returns all parts, laid end to end along the dimension named above; each array names one. Nothing has to cross between parts.
Inputs may be any that keep to these rules, and one draw needn't show every extreme that they name: The first tile_live[r, c] slots of device (r, c) hold its tiles, the rest are ignored; some device of each draw uses all 48 slots. `tile_pos`: among the 48 slots of one device, at most 6 have column blocks owned by any one device of its grid column; in every draw each grid column has a device that owns the column blocks of exactly 6 live slots of every device of that column. `tile_bits`: packed 0/1 adjacency words of 8 bits.
All inputs are finite; a program needn't handle non-finite values.
Results may differ from the reference program's by a relative error of at most 0.0011.
Values may be sent and summed in bfloat16 or wider, within the bound.
A program may use at most 128 MiB of HBM per device.

```python
import math
import jax
import jax.numpy as jnp
from jax import lax

TILE = 512
SRC = 16
BATCHES = 2
TILES_DEV = 48
BLOCKS_DEV = 32
DEPTH = 8
N = 262144
N_ROW = 8
N_COL = 2


def draw_tile_live(key, part):
    key = jax.random.fold_in(key, 11)
    first_key, second_key = jax.random.split(key)
    least = (TILES_DEV + N_ROW - 1) // N_ROW
    shifts = jax.random.randint(first_key, (N_ROW * N_COL,), 0, 4)
    live = jnp.maximum(jnp.right_shift(jnp.full((N_ROW * N_COL,), TILES_DEV, jnp.int32), shifts), least)
    busiest = jax.random.randint(second_key, (), 0, N_ROW * N_COL)
    live = live.at[busiest].set(TILES_DEV)
    return live.reshape(N_ROW, N_COL).astype(jnp.int32)


def draw_tile_pos(key, part):
    key = jax.random.fold_in(key, 5)
    hub_key, order_key, row_key, col_key = jax.random.split(key, 4)
    most = (TILES_DEV + N_ROW - 1) // N_ROW
    shape = (N_ROW, N_COL, TILES_DEV)
    hubs = jax.random.randint(hub_key, (N_COL,), 0, N_ROW)
    order_keys = jax.random.split(order_key, N_ROW * N_COL)
    others = jax.vmap(lambda one_key: jax.random.permutation(one_key, N_ROW - 1))(order_keys)
    others = others.reshape(N_ROW, N_COL, N_ROW - 1).astype(jnp.int32) + 1
    slot_ids = jnp.arange(TILES_DEV, dtype=jnp.int32)
    extra = jnp.maximum(slot_ids - most, 0) % (N_ROW - 1)
    offsets = jnp.take(others, extra, axis=2)
    offsets = jnp.where(slot_ids[None, None, :] < most, 0, offsets)
    owners = (hubs[None, :, None] + offsets) % N_ROW
    row_blocks = jax.random.randint(row_key, shape, 0, N_COL * BLOCKS_DEV)
    locals_ = jax.random.randint(col_key, shape, 0, BLOCKS_DEV)
    return (row_blocks * (N_ROW * BLOCKS_DEV) + owners * BLOCKS_DEV + locals_).astype(jnp.int32)


def draw_tile_bits(key, part):
    key = jax.random.fold_in(key, 7)
    shape = (N_ROW, N_COL, TILES_DEV, TILE // 8, TILE)
    word_keys = jax.random.split(key, 5)
    words = jax.random.randint(word_keys[0], shape, 0, 256, dtype=jnp.int32)
    for word_key in word_keys[1:]:
        words = jnp.bitwise_and(words, jax.random.randint(word_key, shape, 0, 256, dtype=jnp.int32))
    return words


def plant(drawn, own_key, low, high):
    dims = drawn.shape
    place = [jax.random.randint(jax.random.fold_in(own_key, axis), (), 0, dims[axis]) for axis in range(len(dims))]
    drawn = drawn.at[tuple(place)].set(low)
    longest = dims.index(max(dims))
    place[longest] = (place[longest] + 1) % dims[longest]
    return drawn.at[tuple(place)].set(high)


def block_levels(rng, shape, shards, low, largest):
    def one(position, parts):
        draws = jax.random.uniform(jax.random.fold_in(jax.random.fold_in(rng, 6), position), (parts,), jnp.float32, low / len(shards), largest / len(shards))
        return jnp.repeat(jnp.exp(draws), shape[position] // parts).reshape((-1,) + (1,) * (len(shape) - position - 1))

    gain = one(*shards[0])
    for cut in shards[1:]:
        gain = gain * one(*cut)
    return gain


def setup_inputs(seed: int = 0, part: int = 0) -> dict:
    key_list = jax.random.split(jax.random.key(seed), 7)
    part_keys = jax.random.split(jax.random.fold_in(key_list[6], part), 7)
    first_counts = jnp.clip(jnp.exp(math.log(100.0) - 4.6051702 * jax.random.uniform(part_keys[0], (BATCHES, SRC, N), jnp.float32) ** block_levels(part_keys[0], (BATCHES, SRC, N), ((2, 16),), -0.2, 0.2)), 1.0, 100.0).astype(jnp.bfloat16)
    depth = plant(jax.random.randint(part_keys[1], (BATCHES, SRC, N), DEPTH - 2, DEPTH + 1), jax.random.fold_in(part_keys[1], 1), DEPTH - 2, DEPTH).astype(jnp.int32)
    sources = plant(jax.random.randint(part_keys[2], (BATCHES, SRC), 0, N), jax.random.fold_in(part_keys[2], 1), 0, N - 1).astype(jnp.int32)
    tile_pos = draw_tile_pos(jax.random.fold_in(jax.random.fold_in(key_list[6], part), 71), part)
    tile_live = draw_tile_live(jax.random.fold_in(jax.random.fold_in(key_list[6], part), 71), part)
    tile_bits = draw_tile_bits(jax.random.fold_in(jax.random.fold_in(key_list[6], part), 71), part)
    return {"first_counts": first_counts, "depth": depth, "sources": sources, "tile_pos": tile_pos, "tile_live": tile_live, "tile_bits": tile_bits}


def unpack(words):
    shifts = jnp.arange(8, dtype=jnp.int32)
    bits = jnp.bitwise_and(jnp.right_shift(words[:, :, None, :], shifts[None, None, :, None]), 1)
    return bits.reshape(words.shape[0], words.shape[1] * 8, words.shape[2])


def spread(vectors, tile_pos, tile_live, tile_bits, forward):
    rows = vectors.shape[0]
    block_count = N // TILE
    vec_blocks = vectors.reshape(rows, block_count, TILE).astype(jnp.float32)
    total = jnp.zeros((rows, block_count, TILE), jnp.float32)
    slot_ids = jnp.arange(TILES_DEV, dtype=jnp.int32)
    stripe_span = N_ROW * BLOCKS_DEV

    def step(index, total):
        index = jnp.asarray(index).astype(jnp.int32)
        row_dev = index // N_COL
        col_dev = index % N_COL
        places = tile_pos[row_dev, col_dev].astype(jnp.int32)
        row_block = row_dev * (N_COL * BLOCKS_DEV) + places // stripe_span
        column = places % stripe_span
        col_block = ((column // BLOCKS_DEV) * N_COL + col_dev) * BLOCKS_DEV + column % BLOCKS_DEV
        valid = slot_ids < tile_live[row_dev, col_dev]
        tiles = jnp.where(valid[:, None, None], unpack(tile_bits[row_dev, col_dev]), 0).astype(jnp.float32)
        if forward:
            pieces = jnp.take(vec_blocks, row_block, axis=1)
            terms = jnp.einsum("qsu,suv->qsv", pieces, tiles, precision=lax.Precision.HIGHEST)
            return total.at[:, col_block, :].add(terms)
        pieces = jnp.take(vec_blocks, col_block, axis=1)
        terms = jnp.einsum("qsv,suv->qsu", pieces, tiles, precision=lax.Precision.HIGHEST)
        return total.at[:, row_block, :].add(terms)

    total = lax.fori_loop(0, N_ROW * N_COL, step, total)
    return total.reshape(rows, N)


def reference(first_counts, depth, sources, tile_pos, tile_live, tile_bits):
    batch_count, src_count, width = first_counts.shape
    rows = batch_count * src_count
    counts0 = first_counts.astype(jnp.float32).reshape(rows, width)
    levels = depth.reshape(rows, width)
    mask_first = levels == DEPTH - 2
    mask_middle = levels == DEPTH - 1
    mask_last = levels == DEPTH
    zero = jnp.float32(0.0)
    frontier0 = jnp.where(mask_first, counts0, zero).astype(jnp.bfloat16)
    counts1 = jnp.where(mask_middle, spread(frontier0, tile_pos, tile_live, tile_bits, True), zero)
    frontier1 = counts1.astype(jnp.bfloat16)
    counts2 = jnp.where(mask_last, spread(frontier1, tile_pos, tile_live, tile_bits, True), zero)
    weights2 = jnp.where(mask_last, 1.0 / jnp.maximum(counts2, 1.0), zero).astype(jnp.bfloat16)
    delta1 = jnp.where(mask_middle, counts1 * spread(weights2, tile_pos, tile_live, tile_bits, False), zero)
    weights1 = jnp.where(mask_middle, (1.0 + delta1) / jnp.maximum(counts1, 1.0), zero).astype(jnp.bfloat16)
    delta2 = jnp.where(mask_first, counts0 * spread(weights1, tile_pos, tile_live, tile_bits, False), zero)
    dependency = delta1 + delta2
    vertex = jnp.arange(width, dtype=jnp.int32)
    keep = vertex[None, :] != sources.reshape(rows, 1).astype(jnp.int32)
    centrality = jnp.sum(jnp.where(keep, dependency, zero), axis=0)
    return dependency.reshape(batch_count, src_count, width), centrality
```

```python
import jax
import jax.numpy as jnp
from jax import lax
from jax.sharding import PartitionSpec as P

DEPTH = 8
STEPS = 2000.0
CODE_ZERO = -32768


def encode(values):
    code = jnp.round(jnp.log2(jnp.maximum(values, 1.0)) * STEPS).astype(jnp.int32) + (CODE_ZERO + 1)
    return jnp.where(values > 0.0, code, CODE_ZERO).astype(jnp.int16)


def decode(code):
    wide = code.astype(jnp.int32)
    value = jnp.exp2((wide - (CODE_ZERO + 1)).astype(jnp.float32) * (1.0 / STEPS))
    return jnp.where(wide > CODE_ZERO, value, 0.0)


def unpack_tiles(words):
    slot_total, word_count, width = words.shape
    shifts = jnp.arange(8, dtype=jnp.int32)
    bits = jnp.bitwise_and(jnp.right_shift(words[:, :, None, :], shifts[None, None, :, None]), 1)
    return bits.astype(jnp.bfloat16).reshape(slot_total, word_count * 8, width)


def shards(first_counts, depth, sources, tile_pos, tile_live, tile_bits):
    batch_count, src_count, width = first_counts.shape
    row_count = lax.axis_size("row")
    col_count = lax.axis_size("col")
    tile_size = tile_bits.shape[-1]
    slot_total = tile_bits.shape[2]
    blocks = width // tile_size
    most = (slot_total + row_count - 1) // row_count
    seats = row_count * most
    live_count = tile_live.reshape(())
    places = tile_pos.reshape(slot_total)
    stripe_span = row_count * blocks
    row_block = places // stripe_span
    column = places % stripe_span
    owner = column // blocks
    local_block = column % blocks
    slot_ids = jnp.arange(slot_total, dtype=jnp.int32)
    live = slot_ids < live_count
    before = jnp.logical_and(
        owner[:, None] == owner[None, :], slot_ids[None, :] < slot_ids[:, None]
    )
    position = owner * most + jnp.sum(before.astype(jnp.int32), axis=1)
    matched = jnp.logical_and(
        position[None, :] == jnp.arange(seats, dtype=jnp.int32)[:, None], live[None, :]
    )
    filled = jnp.any(matched, axis=1)

    def seat_of(values):
        return jnp.sum(jnp.where(matched, values[None, :], 0), axis=1)

    seat_slot = seat_of(slot_ids)
    seat_row = seat_of(row_block)
    seat_block = jnp.where(filled, seat_of(local_block), blocks)
    arrived = lax.all_to_all(seat_block, "row", split_axis=0, concat_axis=0, tiled=True)
    arrived_valid = arrived < blocks
    arrived_near = jnp.minimum(arrived, blocks - 1)
    block_ids = jnp.arange(blocks, dtype=jnp.int32)
    stripe_ids = jnp.arange(col_count * blocks, dtype=jnp.int32)
    arrived_onehot = (block_ids[:, None] == arrived[None, :]).astype(jnp.float32)
    row_onehot = jnp.logical_and(
        stripe_ids[:, None] == seat_row[None, :], filled[None, :]
    ).astype(jnp.float32)
    words = jnp.take(tile_bits.reshape(slot_total, tile_size // 8, tile_size), seat_slot, axis=0)
    tiles = unpack_tiles(words)

    def exchange(values):
        return lax.all_to_all(values, "row", split_axis=0, concat_axis=0, tiled=True)

    def forward_level(frontier):
        stripe = lax.all_gather(frontier, "col", axis=0, tiled=True)
        pieces = jnp.where(
            filled[:, None, None], jnp.take(stripe, seat_row, axis=0), jnp.zeros((), jnp.bfloat16)
        )
        terms = jnp.einsum("squ,suv->sqv", pieces, tiles, preferred_element_type=jnp.float32)
        received = decode(exchange(encode(terms)))
        return jnp.einsum("es,sqv->eqv", arrived_onehot, received, precision=lax.Precision.HIGHEST)

    def backward_level(weights):
        owned = jnp.take(weights, arrived_near, axis=0)
        outgoing = jnp.where(arrived_valid[:, None, None], owned, jnp.zeros((), jnp.bfloat16))
        pieces = exchange(outgoing)
        terms = jnp.einsum("sqv,suv->squ", pieces, tiles, preferred_element_type=jnp.float32)
        summed = jnp.einsum("as,squ->aqu", row_onehot, terms, precision=lax.Precision.HIGHEST)
        return lax.psum_scatter(summed, "col", scatter_dimension=0, tiled=True)

    zero = jnp.float32(0.0)

    def by_block(values):
        return values.reshape(src_count, blocks, tile_size).transpose(1, 0, 2)

    def chain(first, level):
        levels = by_block(level)
        counts0 = by_block(first).astype(jnp.float32)
        mask_first = levels == DEPTH - 2
        mask_middle = levels == DEPTH - 1
        mask_last = levels == DEPTH
        frontier0 = jnp.where(mask_first, counts0, zero).astype(jnp.bfloat16)
        counts1 = jnp.where(mask_middle, forward_level(frontier0), zero)
        counts2 = jnp.where(mask_last, forward_level(counts1.astype(jnp.bfloat16)), zero)
        weights2 = jnp.where(mask_last, 1.0 / jnp.maximum(counts2, 1.0), zero).astype(jnp.bfloat16)
        delta1 = jnp.where(mask_middle, counts1 * backward_level(weights2), zero)
        weights1 = jnp.where(mask_middle, (1.0 + delta1) / jnp.maximum(counts1, 1.0), zero).astype(
            jnp.bfloat16
        )
        delta2 = jnp.where(mask_first, counts0 * backward_level(weights1), zero)
        return (delta1 + delta2).transpose(1, 0, 2).reshape(src_count, width)

    dependency = jnp.stack([chain(first_counts[b], depth[b]) for b in range(batch_count)])
    offset = (lax.axis_index("row") * col_count + lax.axis_index("col")) * width
    vertex = offset + jnp.arange(width, dtype=jnp.int32)
    keep = vertex[None, None, :] != sources[:, :, None]
    centrality = jnp.sum(jnp.where(keep, dependency, zero), axis=(0, 1))
    return (dependency, centrality)


def solution(mesh):
    placed = (
        P("groups", None, ("row", "col")),
        P("groups", None, ("row", "col")),
        P("groups", None),
        P(("groups", "row"), "col", None),
        P(("groups", "row"), "col"),
        P(("groups", "row"), "col", None, None, None),
    )
    return jax.shard_map(
        shards,
        mesh=mesh,
        in_specs=placed,
        out_specs=(P("groups", None, ("row", "col")), P(("groups", "row", "col"))),
        check_vma=False,
    )
```

```python
import functools

import jax
import jax.numpy as jnp
from jax import lax
from jax.experimental import pallas as pl
from jax.experimental.pallas import tpu as pltpu
from jax.sharding import PartitionSpec as P

DEPTH = 8
STEPS = 2000.0
CODE_ZERO = -32768
MESH = pl.DeviceIdType.MESH


def encode(values):
    code = (jnp.log2(jnp.maximum(values, 1.0)) * STEPS + 0.5).astype(jnp.int32) + (CODE_ZERO + 1)
    return jnp.where(values > 0.0, code, CODE_ZERO).astype(jnp.int16)


def decode(code):
    wide = code.astype(jnp.int32)
    value = jnp.exp2((wide - (CODE_ZERO + 1)).astype(jnp.float32) * (1.0 / STEPS))
    return jnp.where(wide > CODE_ZERO, value, 0.0)


def unpack(words):
    count, width = words.shape
    shifts = lax.broadcasted_iota(jnp.int32, (count, 8, width), 1)
    bits = jnp.bitwise_and(jnp.right_shift(words[:, None, :], shifts), 1)
    return bits.reshape(count * 8, width).astype(jnp.float32).astype(jnp.bfloat16)


def loop(count, body):
    def step(index, carry):
        body(index)
        return carry

    lax.fori_loop(0, count, step, 0)


def kernel(
    layout,
    rows,
    cols,
    most,
    blocks,
    table,
    words,
    first,
    depth,
    sources,
    dependency,
    centrality,
    stripe0,
    stripe1,
    code_out,
    code_in0,
    code_in1,
    weight_out,
    weight_in0,
    weight_in1,
    weights,
    counts1,
    delta1,
    running,
    terms,
    sum_out,
    sum_in,
    code_sent,
    code_got,
    weight_sent,
    weight_got,
    stripe_sent,
    stripe_got,
    sum_sent,
    sum_got,
):
    seats = rows * most
    tile = words.shape[-1]
    stripe = (stripe0, stripe1)
    code_in = (code_in0, code_in1)
    weight_in = (weight_in0, weight_in1)
    row = lax.axis_index("row")
    col = lax.axis_index("col")
    partner = 1 - col

    def entry(name, index):
        return table[layout[name] + index]

    barrier = pltpu.get_barrier_semaphore()

    def greet(step):
        peer = lax.rem(row + step + 1, rows)
        pl.semaphore_signal(barrier, inc=1, device_id={"row": peer}, device_id_type=MESH)

    loop(rows - 1, greet)
    pl.semaphore_signal(barrier, inc=1, device_id={"col": partner}, device_id_type=MESH)

    def lanes(block):
        return pl.ds(pl.multiple_of(block * tile, tile), tile)

    def tile_of(seat):
        return unpack(jnp.bitwise_and(words[entry("slot", seat)], entry("fill", seat)))

    def stripe_copy(level):
        own = pl.ds(col * blocks, blocks)
        return pltpu.make_async_remote_copy(
            src_ref=stripe[level].at[own],
            dst_ref=stripe[level].at[own],
            send_sem=stripe_sent.at[level],
            recv_sem=stripe_got.at[level],
            device_id={"col": partner},
            device_id_type=MESH,
        )

    def stripe_arrival(level):
        other = pl.ds(partner * blocks, blocks)
        return pltpu.make_async_remote_copy(
            src_ref=stripe[level].at[other],
            dst_ref=stripe[level].at[other],
            send_sem=stripe_sent.at[level],
            recv_sem=stripe_got.at[level],
            device_id={"col": partner},
            device_id_type=MESH,
        )

    def seat_copy(out, into, sent, got, level, src_row, dst_row, peer):
        return pltpu.make_async_remote_copy(
            src_ref=out.at[level, pl.ds(dst_row * most, most)],
            dst_ref=into[level].at[pl.ds(src_row * most, most)],
            send_sem=sent.at[level, dst_row],
            recv_sem=got.at[level, src_row],
            device_id={"row": peer},
            device_id_type=MESH,
        )

    def leaving(step):
        return lax.rem(row + step + 1, rows)

    def arriving(step):
        return lax.rem(row + rows - 1 - step, rows)

    def segment_sums(load, order, same):
        def step(index, total):
            carry = total * entry(same, index).astype(jnp.float32)
            total = load(entry(order, index)) + carry
            running[index] = total
            return total

        lax.fori_loop(0, seats, step, jnp.zeros(running.shape[1:], jnp.float32))

    def segment(last, some, block):
        return running[entry(last, block)] * entry(some, block).astype(jnp.float32)

    def forward_level(level, finish):
        stripe_arrival(level).wait_recv()

        def product(seat):
            piece = stripe[level][entry("row", seat)]
            return encode(jnp.dot(piece, tile_of(seat), preferred_element_type=jnp.float32))

        def send(step):
            peer = leaving(step)

            def one(place):
                code_out[level, peer * most + place] = product(peer * most + place)

            loop(most, one)
            seat_copy(code_out, code_in, code_sent, code_got, level, row, peer, peer).start()

        loop(rows - 1, send)

        def own(place):
            code_in[level][row * most + place] = product(row * most + place)

        loop(most, own)

        def arrive(step):
            peer = arriving(step)
            seat_copy(code_out, code_in, code_sent, code_got, level, peer, row, peer).wait_recv()

        loop(rows - 1, arrive)
        segment_sums(lambda seat: decode(code_in[level][seat]), "in_order", "in_same")
        loop(blocks, lambda block: finish(block, segment("in_last", "in_some", block)))

    def backward_level(level, finish):
        def send(step):
            peer = leaving(step)

            def one(place):
                seat = peer * most + place
                weight_out[level, seat] = weights[level, entry("block", seat)]

            loop(most, one)
            seat_copy(weight_out, weight_in, weight_sent, weight_got, level, row, peer, peer).start()

        loop(rows - 1, send)

        def product(seat, piece):
            terms[seat] = lax.dot_general(
                piece, tile_of(seat), (((1,), (1,)), ((), ())), preferred_element_type=jnp.float32
            )

        def own(place):
            seat = row * most + place
            product(seat, weights[level, entry("block", seat)])

        loop(most, own)

        def arrive(step):
            peer = arriving(step)
            seat_copy(
                weight_out, weight_in, weight_sent, weight_got, level, peer, row, peer
            ).wait_recv()

            def one(place):
                seat = peer * most + place
                product(seat, weight_in[level][seat])

            loop(most, one)

        loop(rows - 1, arrive)
        segment_sums(lambda seat: terms[seat], "row_order", "row_same")

        def leave(block):
            sum_out[level, block] = segment("row_last", "row_some", partner * blocks + block)

        loop(blocks, leave)
        copy = pltpu.make_async_remote_copy(
            src_ref=sum_out.at[level],
            dst_ref=sum_in.at[level],
            send_sem=sum_sent.at[level],
            recv_sem=sum_got.at[level],
            device_id={"col": partner},
            device_id_type=MESH,
        )
        copy.start()
        copy.wait_recv()

        def total(block):
            mine = segment("row_last", "row_some", col * blocks + block)
            finish(block, mine + sum_in[level, block])

        loop(blocks, total)
        copy.wait_send()

    def start0(block):
        counts0 = first[:, lanes(block)].astype(jnp.float32)
        masked = jnp.where(depth[:, lanes(block)] == DEPTH - 2, counts0, 0.0)
        stripe0[col * blocks + block] = masked.astype(jnp.bfloat16)

    loop(blocks, start0)
    pl.semaphore_wait(barrier, rows)
    stripe_copy(0).start()

    def finish0(block, total):
        counts = jnp.where(depth[:, lanes(block)] == DEPTH - 1, total, 0.0)
        counts1[block] = counts
        stripe1[col * blocks + block] = counts.astype(jnp.bfloat16)

    forward_level(0, finish0)
    stripe_copy(1).start()

    def finish1(block, total):
        weight = jnp.where(depth[:, lanes(block)] == DEPTH, 1.0 / jnp.maximum(total, 1.0), 0.0)
        weights[0, block] = weight.astype(jnp.bfloat16)

    forward_level(1, finish1)

    def finish2(block, total):
        middle = depth[:, lanes(block)] == DEPTH - 1
        counts = counts1[block]
        delta = jnp.where(middle, counts * total, 0.0)
        delta1[block] = delta
        weight = jnp.where(middle, (1.0 + delta) / jnp.maximum(counts, 1.0), 0.0)
        weights[1, block] = weight.astype(jnp.bfloat16)

    backward_level(0, finish2)
    offset = (row * cols + col) * (blocks * tile)

    def finish3(block, total):
        counts0 = first[:, lanes(block)].astype(jnp.float32)
        delta = jnp.where(depth[:, lanes(block)] == DEPTH - 2, counts0 * total, 0.0)
        value = delta1[block] + delta
        dependency[:, lanes(block)] = value
        vertex = lax.broadcasted_iota(jnp.int32, value.shape, 1) + (offset + block * tile)
        kept = jnp.where(vertex != sources[...], value, 0.0)
        centrality[:, lanes(block)] = jnp.sum(kept, axis=0, keepdims=True)

    backward_level(1, finish3)

    for level in range(2):
        stripe_copy(level).wait_send()

        def sent(step, level=level):
            peer = leaving(step)
            seat_copy(code_out, code_in, code_sent, code_got, level, row, peer, peer).wait_send()
            seat_copy(
                weight_out, weight_in, weight_sent, weight_got, level, row, peer, peer
            ).wait_send()

        loop(rows - 1, sent)


def sorted_runs(keys, kinds):
    seats = keys.shape[0]
    ids = jnp.arange(seats, dtype=jnp.int32)
    ahead = jnp.logical_or(
        keys[None, :] < keys[:, None],
        jnp.logical_and(keys[None, :] == keys[:, None], ids[None, :] < ids[:, None]),
    )
    rank = jnp.sum(ahead.astype(jnp.int32), axis=1)
    placed = rank[None, :] == ids[:, None]
    order = jnp.sum(jnp.where(placed, ids[None, :], 0), axis=1)
    equal_before = jnp.logical_and(keys[None, :] == keys[:, None], ids[None, :] < ids[:, None])
    repeated = jnp.any(equal_before, axis=1)
    same = jnp.sum(jnp.where(placed, repeated[None, :], False).astype(jnp.int32), axis=1)
    kind_ids = jnp.arange(kinds, dtype=jnp.int32)
    upto = jnp.sum((keys[None, :] <= kind_ids[:, None]).astype(jnp.int32), axis=1)
    last = jnp.maximum(upto - 1, 0)
    some = jnp.any(keys[None, :] == kind_ids[:, None], axis=1).astype(jnp.int32)
    return order, same, last, some


def shards(first_counts, depth, sources, tile_pos, tile_live, tile_bits):
    batch_count, src_count, width = first_counts.shape
    row_count = lax.axis_size("row")
    col_count = lax.axis_size("col")
    tile_size = tile_bits.shape[-1]
    slot_total = tile_bits.shape[2]
    row_all = batch_count * src_count
    blocks = width // tile_size
    most = (slot_total + row_count - 1) // row_count
    seats = row_count * most
    live_count = tile_live.reshape(())
    places = tile_pos.reshape(slot_total)
    stripe_span = row_count * blocks
    row_block = places // stripe_span
    column = places % stripe_span
    owner = column // blocks
    local_block = column % blocks
    slot_ids = jnp.arange(slot_total, dtype=jnp.int32)
    before = jnp.logical_and(
        owner[:, None] == owner[None, :], slot_ids[None, :] < slot_ids[:, None]
    )
    position = owner * most + jnp.sum(before.astype(jnp.int32), axis=1)
    matched = jnp.logical_and(
        position[None, :] == jnp.arange(seats, dtype=jnp.int32)[:, None],
        slot_ids[None, :] < live_count,
    )
    filled = jnp.any(matched, axis=1)

    def seat_of(values):
        return jnp.sum(jnp.where(matched, values[None, :], 0), axis=1)

    seat_row = seat_of(row_block)
    seat_block = jnp.where(filled, seat_of(local_block), blocks)
    gathered = lax.all_gather(seat_block, "row", axis=0, tiled=False)
    arrived = lax.dynamic_slice_in_dim(
        gathered, lax.axis_index("row") * most, most, axis=1
    ).reshape(seats)
    in_runs = sorted_runs(arrived, blocks)
    row_runs = sorted_runs(seat_row, col_count * blocks)
    fields = {
        "slot": seat_of(slot_ids),
        "fill": -filled.astype(jnp.int32),
        "row": seat_row,
        "block": jnp.minimum(arrived, blocks - 1),
    }
    for prefix, runs in (("in", in_runs), ("row", row_runs)):
        for name, values in zip(("order", "same", "last", "some"), runs):
            fields[prefix + "_" + name] = values
    layout = {}
    used = 0
    for name, values in fields.items():
        layout[name] = used
        used += values.shape[0]
    table = jnp.concatenate(list(fields.values()))

    vmem = pl.BlockSpec(memory_space=pltpu.VMEM)
    block_shape = (row_all, tile_size)
    dma = pltpu.SemaphoreType.DMA
    scratch = [
        pltpu.VMEM((col_count * blocks,) + block_shape, jnp.bfloat16),
        pltpu.VMEM((col_count * blocks,) + block_shape, jnp.bfloat16),
        pltpu.VMEM((2, seats) + block_shape, jnp.int16),
        pltpu.VMEM((seats,) + block_shape, jnp.int16),
        pltpu.VMEM((seats,) + block_shape, jnp.int16),
        pltpu.VMEM((2, seats) + block_shape, jnp.bfloat16),
        pltpu.VMEM((seats,) + block_shape, jnp.bfloat16),
        pltpu.VMEM((seats,) + block_shape, jnp.bfloat16),
        pltpu.VMEM((2, blocks) + block_shape, jnp.bfloat16),
        pltpu.VMEM((blocks,) + block_shape, jnp.float32),
        pltpu.VMEM((blocks,) + block_shape, jnp.float32),
        pltpu.VMEM((seats,) + block_shape, jnp.float32),
        pltpu.VMEM((seats,) + block_shape, jnp.float32),
        pltpu.VMEM((2, blocks) + block_shape, jnp.float32),
        pltpu.VMEM((2, blocks) + block_shape, jnp.float32),
        dma((2, row_count)),
        dma((2, row_count)),
        dma((2, row_count)),
        dma((2, row_count)),
        dma((2,)),
        dma((2,)),
        dma((2,)),
        dma((2,)),
    ]
    dependency, centrality = pl.pallas_call(
        functools.partial(kernel, layout, row_count, col_count, most, blocks),
        out_shape=(
            jax.ShapeDtypeStruct((row_all, width), jnp.float32),
            jax.ShapeDtypeStruct((1, width), jnp.float32),
        ),
        in_specs=[pl.BlockSpec(memory_space=pltpu.SMEM), vmem, vmem, vmem, vmem],
        out_specs=(vmem, vmem),
        scratch_shapes=scratch,
        compiler_params=pltpu.CompilerParams(
            collective_id=0, has_side_effects=True, vmem_limit_bytes=60 * 1024 * 1024
        ),
        cost_estimate=pl.CostEstimate(
            flops=8 * seats * row_all * tile_size * tile_size,
            bytes_accessed=4 * tile_bits.size + 16 * row_all * width,
            transcendentals=4 * seats * row_all * tile_size,
        ),
    )(
        table,
        tile_bits.reshape(slot_total, tile_size // 8, tile_size),
        first_counts.reshape(row_all, width),
        depth.reshape(row_all, width),
        sources.reshape(row_all, 1),
    )
    return dependency.reshape(batch_count, src_count, width), centrality.reshape(width)


def solution(mesh):
    placed = (
        P("groups", None, ("row", "col")),
        P("groups", None, ("row", "col")),
        P("groups", None),
        P(("groups", "row"), "col", None),
        P(("groups", "row"), "col"),
        P(("groups", "row"), "col", None, None, None),
    )
    return jax.shard_map(
        shards,
        mesh=mesh,
        in_specs=placed,
        out_specs=(P("groups", None, ("row", "col")), P(("groups", "row", "col"))),
        check_vma=False,
    )
```

```python
import functools

import jax
import jax.numpy as jnp
from jax import lax
from jax.experimental import pallas as pl
from jax.experimental.pallas import tpu as pltpu
from jax.sharding import PartitionSpec as P

DEPTH = 8
STEPS = 2000.0
CODE_ZERO = -32768
MESH = pl.DeviceIdType.MESH


def encode(values):
    code = (jnp.log2(jnp.maximum(values, 1.0)) * STEPS + 0.5).astype(jnp.int32) + (CODE_ZERO + 1)
    return jnp.where(values > 0.0, code, CODE_ZERO).astype(jnp.int16)


def decode(code):
    wide = code.astype(jnp.int32)
    value = jnp.exp2((wide - (CODE_ZERO + 1)).astype(jnp.float32) * (1.0 / STEPS))
    return jnp.where(wide > CODE_ZERO, value, 0.0)


def unpack(words):
    count, width = words.shape
    shifts = lax.broadcasted_iota(jnp.int32, (count, 8, width), 1)
    bits = jnp.bitwise_and(jnp.right_shift(words[:, None, :], shifts), 1)
    return bits.reshape(count * 8, width).astype(jnp.float32).astype(jnp.bfloat16)


def loop(count, body):
    def step(index, carry):
        body(index)
        return carry

    lax.fori_loop(0, count, step, 0)


def gather_kernel(rows, mine, result, landed, sent, got):
    row = lax.axis_index("row")
    barrier = pltpu.get_barrier_semaphore()

    def greet(step):
        peer = lax.rem(row + step + 1, rows)
        pl.semaphore_signal(barrier, inc=1, device_id={"row": peer}, device_id_type=MESH)

    loop(rows - 1, greet)
    pl.semaphore_wait(barrier, rows - 1)

    def copy(source, target):
        return pltpu.make_async_remote_copy(
            src_ref=mine,
            dst_ref=landed.at[source],
            send_sem=sent.at[target],
            recv_sem=got.at[source],
            device_id={"row": target},
            device_id_type=MESH,
        )

    loop(rows - 1, lambda step: copy(row, lax.rem(row + step + 1, rows)).start())
    landed[row] = mine[...]

    def arrive(step):
        peer = lax.rem(row + step + 1, rows)
        copy(peer, peer).wait_recv()

    loop(rows - 1, arrive)
    result[...] = landed[...]
    loop(rows - 1, lambda step: copy(row, lax.rem(row + step + 1, rows)).wait_send())


def gather_rows(values, rows):
    lanes = (values.shape[0] + 127) // 128 * 128
    padded = jnp.broadcast_to(jnp.pad(values, (0, lanes - values.shape[0]))[None, :], (8, lanes))
    vmem = pl.BlockSpec(memory_space=pltpu.VMEM)
    gathered = pl.pallas_call(
        functools.partial(gather_kernel, rows),
        out_shape=jax.ShapeDtypeStruct((rows, 8, lanes), values.dtype),
        in_specs=[vmem],
        out_specs=vmem,
        scratch_shapes=[
            pltpu.VMEM((rows, 8, lanes), values.dtype),
            pltpu.SemaphoreType.DMA((rows,)),
            pltpu.SemaphoreType.DMA((rows,)),
        ],
        compiler_params=pltpu.CompilerParams(collective_id=1, has_side_effects=True),
    )(padded)
    return gathered[:, 0, :]


def kernel(
    layout,
    rows,
    cols,
    most,
    blocks,
    table,
    words,
    first,
    depth,
    sources,
    dependency,
    centrality,
    stripe,
    code_out,
    code_in,
    weight_out,
    weight_in,
    weights,
    sum_out,
    sum_in,
    counts1,
    delta1,
    running,
    terms,
    code_sent,
    code_got,
    weight_sent,
    weight_got,
    stripe_sent,
    stripe_got,
    sum_sent,
    sum_got,
):
    seats = rows * most
    tile = words.shape[-1]
    half_rows = running.shape[1]
    row = lax.axis_index("row")
    col = lax.axis_index("col")
    partner = 1 - col

    def entry(name, index):
        return table[layout[name] + index]

    barrier = pltpu.get_barrier_semaphore()

    def leaving(step):
        return lax.rem(row + step + 1, rows)

    def arriving(step):
        return lax.rem(row + rows - 1 - step, rows)

    def greet(step):
        pl.semaphore_signal(barrier, inc=1, device_id={"row": leaving(step)}, device_id_type=MESH)

    loop(rows - 1, greet)
    pl.semaphore_signal(barrier, inc=1, device_id={"col": partner}, device_id_type=MESH)

    def lanes(block):
        return pl.ds(pl.multiple_of(block * tile, tile), tile)

    def view(ref, half, block):
        return ref[half * half_rows : (half + 1) * half_rows, lanes(block)]

    def tile_of(seat):
        return unpack(jnp.bitwise_and(words[entry("slot", seat)], entry("fill", seat)))

    def stripe_copy(chain, owner):
        part = pl.ds(owner * blocks, blocks)
        return pltpu.make_async_remote_copy(
            src_ref=stripe[chain].at[part],
            dst_ref=stripe[chain].at[part],
            send_sem=stripe_sent.at[chain],
            recv_sem=stripe_got.at[chain],
            device_id={"col": partner},
            device_id_type=MESH,
        )

    def seat_copy(out, into, sent, got, chain, src_row, dst_row, peer):
        return pltpu.make_async_remote_copy(
            src_ref=out[chain].at[pl.ds(dst_row * most, most)],
            dst_ref=into[chain].at[pl.ds(src_row * most, most)],
            send_sem=sent.at[chain, dst_row],
            recv_sem=got.at[chain, src_row],
            device_id={"row": peer},
            device_id_type=MESH,
        )

    def code_copy(chain, src_row, dst_row, peer):
        return seat_copy(code_out, code_in, code_sent, code_got, chain, src_row, dst_row, peer)

    def weight_copy(chain, src_row, dst_row, peer):
        return seat_copy(
            weight_out, weight_in, weight_sent, weight_got, chain, src_row, dst_row, peer
        )

    def sum_copy(chain):
        return pltpu.make_async_remote_copy(
            src_ref=sum_out[chain],
            dst_ref=sum_in[chain],
            send_sem=sum_sent.at[chain],
            recv_sem=sum_got.at[chain],
            device_id={"col": partner},
            device_id_type=MESH,
        )

    def segment_sums(load, order, same):
        def step(index, total):
            carry = total * entry(same, index).astype(jnp.float32)
            total = load(entry(order, index)) + carry
            running[index] = total
            return total

        lax.fori_loop(0, seats, step, jnp.zeros(running.shape[1:], jnp.float32))

    def segment(last, some, block):
        return running[entry(last, block)] * entry(some, block).astype(jnp.float32)

    def forward_send(chain):
        stripe_copy(chain, partner).wait_recv()

        def product(seat):
            piece = stripe[chain][entry("row", seat)]
            return encode(jnp.dot(piece, tile_of(seat), preferred_element_type=jnp.float32))

        def send(step):
            peer = leaving(step)

            def one(place):
                code_out[chain][peer * most + place] = product(peer * most + place)

            loop(most, one)
            code_copy(chain, row, peer, peer).start()

        loop(rows - 1, send)

        def own(place):
            code_in[chain][row * most + place] = product(row * most + place)

        loop(most, own)

    def forward_sum(chain, finish):
        def arrive(step):
            peer = arriving(step)
            code_copy(chain, peer, row, peer).wait_recv()

        loop(rows - 1, arrive)
        segment_sums(lambda seat: decode(code_in[chain][seat]), "in_order", "in_same")
        loop(blocks, lambda block: finish(block, segment("in_last", "in_some", block)))

    def backward_send(chain):
        def send(step):
            peer = leaving(step)

            def one(place):
                seat = peer * most + place
                weight_out[chain][seat] = weights[chain][entry("block", seat)]

            loop(most, one)
            weight_copy(chain, row, peer, peer).start()

        loop(rows - 1, send)

    def backward_sum(chain, finish):
        def product(seat, piece):
            terms[seat] = lax.dot_general(
                piece, tile_of(seat), (((1,), (1,)), ((), ())), preferred_element_type=jnp.float32
            )

        def own(place):
            seat = row * most + place
            product(seat, weights[chain][entry("block", seat)])

        loop(most, own)

        def arrive(step):
            peer = arriving(step)
            weight_copy(chain, peer, row, peer).wait_recv()

            def one(place):
                seat = peer * most + place
                product(seat, weight_in[chain][seat])

            loop(most, one)

        loop(rows - 1, arrive)
        segment_sums(lambda seat: terms[seat], "row_order", "row_same")

        def leave(block):
            sum_out[chain][block] = segment("row_last", "row_some", partner * blocks + block)

        loop(blocks, leave)
        sum_copy(chain).start()
        sum_copy(chain).wait_recv()

        def total(block):
            mine = segment("row_last", "row_some", col * blocks + block)
            finish(block, mine + sum_in[chain][block])

        loop(blocks, total)

    def start(half):
        def one(block):
            counts0 = view(first, half, block).astype(jnp.float32)
            masked = jnp.where(view(depth, half, block) == DEPTH - 2, counts0, 0.0)
            stripe[half][col * blocks + block] = masked.astype(jnp.bfloat16)

        loop(blocks, one)

    def middle_counts(half, block, total):
        counts = jnp.where(view(depth, half, block) == DEPTH - 1, total, 0.0)
        counts1[half, block] = counts
        stripe[2 + half][col * blocks + block] = counts.astype(jnp.bfloat16)

    def last_weights(half, block, total):
        last = view(depth, half, block) == DEPTH
        weight = jnp.where(last, 1.0 / jnp.maximum(total, 1.0), 0.0)
        weights[half][block] = weight.astype(jnp.bfloat16)

    def middle_weights(half, block, total):
        middle = view(depth, half, block) == DEPTH - 1
        counts = counts1[half, block]
        delta = jnp.where(middle, counts * total, 0.0)
        delta1[half, block] = delta
        weight = jnp.where(middle, (1.0 + delta) / jnp.maximum(counts, 1.0), 0.0)
        weights[2 + half][block] = weight.astype(jnp.bfloat16)

    offset = (row * cols + col) * (blocks * tile)

    def results(half, block, total):
        counts0 = view(first, half, block).astype(jnp.float32)
        delta = jnp.where(view(depth, half, block) == DEPTH - 2, counts0 * total, 0.0)
        value = delta1[half, block] + delta
        mine = slice(half * half_rows, (half + 1) * half_rows)
        dependency[mine, lanes(block)] = value
        vertex = lax.broadcasted_iota(jnp.int32, value.shape, 1) + (offset + block * tile)
        kept = jnp.where(vertex != sources[mine, :], value, 0.0)
        part = jnp.sum(kept, axis=0, keepdims=True)
        if half == 0:
            centrality[:, lanes(block)] = part
        else:
            centrality[:, lanes(block)] = centrality[:, lanes(block)] + part

    halves = (0, 1)
    for half in halves:
        start(half)
        if half == 0:
            pl.semaphore_wait(barrier, rows)
        stripe_copy(half, col).start()
    for half in halves:
        forward_send(half)
    for half in halves:
        forward_sum(half, functools.partial(middle_counts, half))
        stripe_copy(2 + half, col).start()
        forward_send(2 + half)
    for half in halves:
        forward_sum(2 + half, functools.partial(last_weights, half))
        backward_send(half)
    for half in halves:
        backward_sum(half, functools.partial(middle_weights, half))
        backward_send(2 + half)
    for half in halves:
        backward_sum(2 + half, functools.partial(results, half))

    for chain in range(4):
        stripe_copy(chain, col).wait_send()
        sum_copy(chain).wait_send()

        def sent(step, chain=chain):
            peer = leaving(step)
            code_copy(chain, row, peer, peer).wait_send()
            weight_copy(chain, row, peer, peer).wait_send()

        loop(rows - 1, sent)


def sorted_runs(keys, kinds):
    seats = keys.shape[0]
    ids = jnp.arange(seats, dtype=jnp.int32)
    ahead = jnp.logical_or(
        keys[None, :] < keys[:, None],
        jnp.logical_and(keys[None, :] == keys[:, None], ids[None, :] < ids[:, None]),
    )
    rank = jnp.sum(ahead.astype(jnp.int32), axis=1)
    placed = rank[None, :] == ids[:, None]
    order = jnp.sum(jnp.where(placed, ids[None, :], 0), axis=1)
    equal_before = jnp.logical_and(keys[None, :] == keys[:, None], ids[None, :] < ids[:, None])
    repeated = jnp.any(equal_before, axis=1)
    same = jnp.sum(jnp.where(placed, repeated[None, :], False).astype(jnp.int32), axis=1)
    kind_ids = jnp.arange(kinds, dtype=jnp.int32)
    upto = jnp.sum((keys[None, :] <= kind_ids[:, None]).astype(jnp.int32), axis=1)
    last = jnp.maximum(upto - 1, 0)
    some = jnp.any(keys[None, :] == kind_ids[:, None], axis=1).astype(jnp.int32)
    return order, same, last, some


def shards(first_counts, depth, sources, tile_pos, tile_live, tile_bits):
    batch_count, src_count, width = first_counts.shape
    row_count = lax.axis_size("row")
    col_count = lax.axis_size("col")
    tile_size = tile_bits.shape[-1]
    slot_total = tile_bits.shape[2]
    row_all = batch_count * src_count
    blocks = width // tile_size
    most = (slot_total + row_count - 1) // row_count
    seats = row_count * most
    live_count = tile_live.reshape(())
    places = tile_pos.reshape(slot_total)
    stripe_span = row_count * blocks
    row_block = places // stripe_span
    column = places % stripe_span
    owner = column // blocks
    local_block = column % blocks
    slot_ids = jnp.arange(slot_total, dtype=jnp.int32)
    before = jnp.logical_and(
        owner[:, None] == owner[None, :], slot_ids[None, :] < slot_ids[:, None]
    )
    position = owner * most + jnp.sum(before.astype(jnp.int32), axis=1)
    matched = jnp.logical_and(
        position[None, :] == jnp.arange(seats, dtype=jnp.int32)[:, None],
        slot_ids[None, :] < live_count,
    )
    filled = jnp.any(matched, axis=1)

    def seat_of(values):
        return jnp.sum(jnp.where(matched, values[None, :], 0), axis=1)

    seat_row = seat_of(row_block)
    seat_block = jnp.where(filled, seat_of(local_block), blocks)
    gathered = gather_rows(seat_block, row_count)
    arrived = lax.dynamic_slice_in_dim(
        gathered, lax.axis_index("row") * most, most, axis=1
    ).reshape(seats)
    in_runs = sorted_runs(arrived, blocks)
    row_runs = sorted_runs(seat_row, col_count * blocks)
    fields = {
        "slot": seat_of(slot_ids),
        "fill": -filled.astype(jnp.int32),
        "row": seat_row,
        "block": jnp.minimum(arrived, blocks - 1),
    }
    for prefix, runs in (("in", in_runs), ("row", row_runs)):
        for name, values in zip(("order", "same", "last", "some"), runs):
            fields[prefix + "_" + name] = values
    layout = {}
    used = 0
    for name, values in fields.items():
        layout[name] = used
        used += values.shape[0]
    table = jnp.concatenate(list(fields.values()))

    vmem = pl.BlockSpec(memory_space=pltpu.VMEM)
    half_shape = (row_all // 2, tile_size)
    dma = pltpu.SemaphoreType.DMA

    def chains(count, dtype):
        return tuple(pltpu.VMEM((count,) + half_shape, dtype) for _ in range(4))

    scratch = [
        chains(col_count * blocks, jnp.bfloat16),
        chains(seats, jnp.int16),
        chains(seats, jnp.int16),
        chains(seats, jnp.bfloat16),
        chains(seats, jnp.bfloat16),
        chains(blocks, jnp.bfloat16),
        chains(blocks, jnp.float32),
        chains(blocks, jnp.float32),
        pltpu.VMEM((2, blocks) + half_shape, jnp.float32),
        pltpu.VMEM((2, blocks) + half_shape, jnp.float32),
        pltpu.VMEM((seats,) + half_shape, jnp.float32),
        pltpu.VMEM((seats,) + half_shape, jnp.float32),
        dma((4, row_count)),
        dma((4, row_count)),
        dma((4, row_count)),
        dma((4, row_count)),
        dma((4,)),
        dma((4,)),
        dma((4,)),
        dma((4,)),
    ]
    dependency, centrality = pl.pallas_call(
        functools.partial(kernel, layout, row_count, col_count, most, blocks),
        out_shape=(
            jax.ShapeDtypeStruct((row_all, width), jnp.float32),
            jax.ShapeDtypeStruct((1, width), jnp.float32),
        ),
        in_specs=[pl.BlockSpec(memory_space=pltpu.SMEM), vmem, vmem, vmem, vmem],
        out_specs=(vmem, vmem),
        scratch_shapes=scratch,
        compiler_params=pltpu.CompilerParams(
            collective_id=0, has_side_effects=True, vmem_limit_bytes=60 * 1024 * 1024
        ),
        cost_estimate=pl.CostEstimate(
            flops=8 * seats * row_all * tile_size * tile_size,
            bytes_accessed=4 * tile_bits.size + 16 * row_all * width,
            transcendentals=4 * seats * row_all * tile_size,
        ),
    )(
        table,
        tile_bits.reshape(slot_total, tile_size // 8, tile_size),
        first_counts.reshape(row_all, width),
        depth.reshape(row_all, width),
        sources.reshape(row_all, 1),
    )
    return dependency.reshape(batch_count, src_count, width), centrality.reshape(width)


def solution(mesh):
    placed = (
        P("groups", None, ("row", "col")),
        P("groups", None, ("row", "col")),
        P("groups", None),
        P(("groups", "row"), "col", None),
        P(("groups", "row"), "col"),
        P(("groups", "row"), "col", None, None, None),
    )
    return jax.shard_map(
        shards,
        mesh=mesh,
        in_specs=placed,
        out_specs=(P("groups", None, ("row", "col")), P(("groups", "row", "col"))),
        check_vma=False,
    )
```

```python
import functools

import jax
import jax.numpy as jnp
from jax import lax
from jax.experimental import pallas as pl
from jax.experimental.pallas import tpu as pltpu
from jax.sharding import PartitionSpec as P

DEPTH = 8
STEPS = 2000.0
CODE_ZERO = -32768
MESH = pl.DeviceIdType.MESH


def encode(values):
    code = (jnp.log2(jnp.maximum(values, 1.0)) * STEPS + 0.5).astype(jnp.int32) + (CODE_ZERO + 1)
    return jnp.where(values > 0.0, code, CODE_ZERO).astype(jnp.int16)


def decode(code):
    wide = code.astype(jnp.int32)
    value = jnp.exp2((wide - (CODE_ZERO + 1)).astype(jnp.float32) * (1.0 / STEPS))
    return jnp.where(wide > CODE_ZERO, value, 0.0)


def unpack(words):
    count, width = words.shape
    shifts = lax.broadcasted_iota(jnp.int32, (count, 8, width), 1)
    bits = jnp.bitwise_and(jnp.right_shift(words[:, None, :], shifts), 1)
    return bits.reshape(count * 8, width).astype(jnp.float32).astype(jnp.bfloat16)


def loop(count, body):
    def step(index, carry):
        body(index)
        return carry

    lax.fori_loop(0, count, step, 0)


def divisor(count, most):
    return max(part for part in range(1, most + 1) if count % part == 0)


def grouped(count, size, compute, store):
    def body(group):
        indices = [group * size + place for place in range(size)]
        values = [compute(index) for index in indices]
        for index, value in zip(indices, values):
            store(index, value)

    if count == size:
        body(0)
    else:
        loop(count // size, body)


def gather_kernel(rows, mine, result, landed, sent, got):
    row = lax.axis_index("row")
    barrier = pltpu.get_barrier_semaphore()

    def greet(step):
        peer = lax.rem(row + step + 1, rows)
        pl.semaphore_signal(barrier, inc=1, device_id={"row": peer}, device_id_type=MESH)

    loop(rows - 1, greet)
    pl.semaphore_wait(barrier, rows - 1)

    def copy(source, target):
        return pltpu.make_async_remote_copy(
            src_ref=mine,
            dst_ref=landed.at[source],
            send_sem=sent.at[target],
            recv_sem=got.at[source],
            device_id={"row": target},
            device_id_type=MESH,
        )

    loop(rows - 1, lambda step: copy(row, lax.rem(row + step + 1, rows)).start())
    landed[row] = mine[...]

    def arrive(step):
        peer = lax.rem(row + step + 1, rows)
        copy(peer, peer).wait_recv()

    loop(rows - 1, arrive)
    result[...] = landed[...]
    loop(rows - 1, lambda step: copy(row, lax.rem(row + step + 1, rows)).wait_send())


def gather_rows(values, rows):
    lanes = (values.shape[0] + 127) // 128 * 128
    padded = jnp.broadcast_to(jnp.pad(values, (0, lanes - values.shape[0]))[None, :], (8, lanes))
    vmem = pl.BlockSpec(memory_space=pltpu.VMEM)
    gathered = pl.pallas_call(
        functools.partial(gather_kernel, rows),
        out_shape=jax.ShapeDtypeStruct((rows, 8, lanes), values.dtype),
        in_specs=[vmem],
        out_specs=vmem,
        scratch_shapes=[
            pltpu.VMEM((rows, 8, lanes), values.dtype),
            pltpu.SemaphoreType.DMA((rows,)),
            pltpu.SemaphoreType.DMA((rows,)),
        ],
        compiler_params=pltpu.CompilerParams(collective_id=1, has_side_effects=True),
    )(padded)
    return gathered[:, 0, :]


def kernel(
    layout,
    rows,
    cols,
    most,
    blocks,
    table,
    words,
    first,
    depth,
    sources,
    dependency,
    centrality,
    stripe,
    code_out,
    code_in,
    weight_out,
    weight_in,
    weights,
    sum_out,
    sum_in,
    counts1,
    delta1,
    running,
    terms,
    code_sent,
    code_got,
    weight_sent,
    weight_got,
    stripe_sent,
    stripe_got,
    sum_sent,
    sum_got,
):
    seats = rows * most
    tile = words.shape[-1]
    half_rows = running.shape[1]
    several = divisor(most, 2)
    some_blocks = divisor(blocks, 4)
    row = lax.axis_index("row")
    col = lax.axis_index("col")
    partner = 1 - col

    def entry(name, index):
        return table[layout[name] + index]

    barrier = pltpu.get_barrier_semaphore()

    def leaving(step):
        return lax.rem(row + step + 1, rows)

    def arriving(step):
        return lax.rem(row + rows - 1 - step, rows)

    def greet(step):
        pl.semaphore_signal(barrier, inc=1, device_id={"row": leaving(step)}, device_id_type=MESH)

    loop(rows - 1, greet)
    pl.semaphore_signal(barrier, inc=1, device_id={"col": partner}, device_id_type=MESH)

    def lanes(block):
        return pl.ds(pl.multiple_of(block * tile, tile), tile)

    def view(ref, half, block):
        return ref[half * half_rows : (half + 1) * half_rows, lanes(block)]

    def tile_of(seat):
        return unpack(jnp.bitwise_and(words[entry("slot", seat)], entry("fill", seat)))

    def stripe_copy(chain, owner):
        part = pl.ds(owner * blocks, blocks)
        return pltpu.make_async_remote_copy(
            src_ref=stripe[chain].at[part],
            dst_ref=stripe[chain].at[part],
            send_sem=stripe_sent.at[chain],
            recv_sem=stripe_got.at[chain],
            device_id={"col": partner},
            device_id_type=MESH,
        )

    def seat_copy(out, into, sent, got, chain, src_row, dst_row, peer):
        return pltpu.make_async_remote_copy(
            src_ref=out[chain].at[pl.ds(dst_row * most, most)],
            dst_ref=into[chain].at[pl.ds(src_row * most, most)],
            send_sem=sent.at[chain, dst_row],
            recv_sem=got.at[chain, src_row],
            device_id={"row": peer},
            device_id_type=MESH,
        )

    def code_copy(chain, src_row, dst_row, peer):
        return seat_copy(code_out, code_in, code_sent, code_got, chain, src_row, dst_row, peer)

    def weight_copy(chain, src_row, dst_row, peer):
        return seat_copy(
            weight_out, weight_in, weight_sent, weight_got, chain, src_row, dst_row, peer
        )

    def sum_copy(chain):
        return pltpu.make_async_remote_copy(
            src_ref=sum_out[chain],
            dst_ref=sum_in[chain],
            send_sem=sum_sent.at[chain],
            recv_sem=sum_got.at[chain],
            device_id={"col": partner},
            device_id_type=MESH,
        )

    def segment_sums(load, order, same):
        size = divisor(seats, 8)

        def group(number, total):
            indices = [number * size + place for place in range(size)]
            loaded = [load(entry(order, index)) for index in indices]
            totals = []
            for index, value in zip(indices, loaded):
                total = total * entry(same, index).astype(jnp.float32) + value
                totals.append(total)
            for index, value in zip(indices, totals):
                running[index] = value
            return total

        lax.fori_loop(0, seats // size, group, jnp.zeros(running.shape[1:], jnp.float32))

    def segment(last, some, block):
        return running[entry(last, block)] * entry(some, block).astype(jnp.float32)

    def forward_send(chain):
        stripe_copy(chain, partner).wait_recv()

        def product(seat):
            piece = stripe[chain][entry("row", seat)]
            return encode(jnp.dot(piece, tile_of(seat), preferred_element_type=jnp.float32))

        def send(step):
            peer = leaving(step)

            def keep(place, value):
                code_out[chain][peer * most + place] = value

            grouped(most, several, lambda place: product(peer * most + place), keep)
            code_copy(chain, row, peer, peer).start()

        loop(rows - 1, send)

        def own(place, value):
            code_in[chain][row * most + place] = value

        grouped(most, several, lambda place: product(row * most + place), own)

    def forward_sum(chain, finish):
        def arrive(step):
            peer = arriving(step)
            code_copy(chain, peer, row, peer).wait_recv()

        loop(rows - 1, arrive)
        segment_sums(lambda seat: decode(code_in[chain][seat]), "in_order", "in_same")
        grouped(blocks, some_blocks, lambda block: segment("in_last", "in_some", block), finish)

    def backward_send(chain):
        def owned(seat):
            return weights[chain][entry("block", seat)]

        def send(step):
            peer = leaving(step)

            def keep(place, value):
                weight_out[chain][peer * most + place] = value

            grouped(most, several, lambda place: owned(peer * most + place), keep)
            weight_copy(chain, row, peer, peer).start()

        loop(rows - 1, send)

    def backward_sum(chain, finish):
        def product(seat, piece):
            return lax.dot_general(
                piece, tile_of(seat), (((1,), (1,)), ((), ())), preferred_element_type=jnp.float32
            )

        def products(peer, piece):
            def keep(place, value):
                terms[peer * most + place] = value

            def one(place):
                return product(peer * most + place, piece(peer * most + place))

            grouped(most, several, one, keep)

        products(row, lambda seat: weights[chain][entry("block", seat)])

        def arrive(step):
            peer = arriving(step)
            weight_copy(chain, peer, row, peer).wait_recv()
            products(peer, lambda seat: weight_in[chain][seat])

        loop(rows - 1, arrive)
        segment_sums(lambda seat: terms[seat], "row_order", "row_same")

        def leaves(block):
            return segment("row_last", "row_some", partner * blocks + block)

        def leave(block, value):
            sum_out[chain][block] = value

        grouped(blocks, some_blocks, leaves, leave)
        sum_copy(chain).start()
        sum_copy(chain).wait_recv()

        def total(block):
            mine = segment("row_last", "row_some", col * blocks + block)
            return mine + sum_in[chain][block]

        grouped(blocks, some_blocks, total, finish)

    def start(half):
        def masked(block):
            counts0 = view(first, half, block).astype(jnp.float32)
            values = jnp.where(view(depth, half, block) == DEPTH - 2, counts0, 0.0)
            return values.astype(jnp.bfloat16)

        def keep(block, value):
            stripe[half][col * blocks + block] = value

        grouped(blocks, some_blocks, masked, keep)

    def middle_counts(half, block, total):
        counts = jnp.where(view(depth, half, block) == DEPTH - 1, total, 0.0)
        counts1[half, block] = counts
        stripe[2 + half][col * blocks + block] = counts.astype(jnp.bfloat16)

    def last_weights(half, block, total):
        last = view(depth, half, block) == DEPTH
        weight = jnp.where(last, 1.0 / jnp.maximum(total, 1.0), 0.0)
        weights[half][block] = weight.astype(jnp.bfloat16)

    def middle_weights(half, block, total):
        middle = view(depth, half, block) == DEPTH - 1
        counts = counts1[half, block]
        delta = jnp.where(middle, counts * total, 0.0)
        delta1[half, block] = delta
        weight = jnp.where(middle, (1.0 + delta) / jnp.maximum(counts, 1.0), 0.0)
        weights[2 + half][block] = weight.astype(jnp.bfloat16)

    offset = (row * cols + col) * (blocks * tile)

    def results(half, block, total):
        counts0 = view(first, half, block).astype(jnp.float32)
        delta = jnp.where(view(depth, half, block) == DEPTH - 2, counts0 * total, 0.0)
        value = delta1[half, block] + delta
        mine = slice(half * half_rows, (half + 1) * half_rows)
        dependency[mine, lanes(block)] = value
        vertex = lax.broadcasted_iota(jnp.int32, value.shape, 1) + (offset + block * tile)
        kept = jnp.where(vertex != sources[mine, :], value, 0.0)
        part = jnp.sum(kept, axis=0, keepdims=True)
        if half == 0:
            centrality[:, lanes(block)] = part
        else:
            centrality[:, lanes(block)] = centrality[:, lanes(block)] + part

    halves = (0, 1)
    for half in halves:
        start(half)
        if half == 0:
            pl.semaphore_wait(barrier, rows)
        stripe_copy(half, col).start()
    for half in halves:
        forward_send(half)
    for half in halves:
        forward_sum(half, functools.partial(middle_counts, half))
        stripe_copy(2 + half, col).start()
        forward_send(2 + half)
    for half in halves:
        forward_sum(2 + half, functools.partial(last_weights, half))
        backward_send(half)
    for half in halves:
        backward_sum(half, functools.partial(middle_weights, half))
        backward_send(2 + half)
    for half in halves:
        backward_sum(2 + half, functools.partial(results, half))

    for chain in range(4):
        stripe_copy(chain, col).wait_send()
        sum_copy(chain).wait_send()

        def sent(step, chain=chain):
            peer = leaving(step)
            code_copy(chain, row, peer, peer).wait_send()
            weight_copy(chain, row, peer, peer).wait_send()

        loop(rows - 1, sent)


def sorted_runs(keys, kinds):
    seats = keys.shape[0]
    ids = jnp.arange(seats, dtype=jnp.int32)
    ahead = jnp.logical_or(
        keys[None, :] < keys[:, None],
        jnp.logical_and(keys[None, :] == keys[:, None], ids[None, :] < ids[:, None]),
    )
    rank = jnp.sum(ahead.astype(jnp.int32), axis=1)
    placed = rank[None, :] == ids[:, None]
    order = jnp.sum(jnp.where(placed, ids[None, :], 0), axis=1)
    equal_before = jnp.logical_and(keys[None, :] == keys[:, None], ids[None, :] < ids[:, None])
    repeated = jnp.any(equal_before, axis=1)
    same = jnp.sum(jnp.where(placed, repeated[None, :], False).astype(jnp.int32), axis=1)
    kind_ids = jnp.arange(kinds, dtype=jnp.int32)
    upto = jnp.sum((keys[None, :] <= kind_ids[:, None]).astype(jnp.int32), axis=1)
    last = jnp.maximum(upto - 1, 0)
    some = jnp.any(keys[None, :] == kind_ids[:, None], axis=1).astype(jnp.int32)
    return order, same, last, some


def shards(first_counts, depth, sources, tile_pos, tile_live, tile_bits):
    batch_count, src_count, width = first_counts.shape
    row_count = lax.axis_size("row")
    col_count = lax.axis_size("col")
    tile_size = tile_bits.shape[-1]
    slot_total = tile_bits.shape[2]
    row_all = batch_count * src_count
    blocks = width // tile_size
    most = (slot_total + row_count - 1) // row_count
    seats = row_count * most
    live_count = tile_live.reshape(())
    places = tile_pos.reshape(slot_total)
    stripe_span = row_count * blocks
    row_block = places // stripe_span
    column = places % stripe_span
    owner = column // blocks
    local_block = column % blocks
    slot_ids = jnp.arange(slot_total, dtype=jnp.int32)
    before = jnp.logical_and(
        owner[:, None] == owner[None, :], slot_ids[None, :] < slot_ids[:, None]
    )
    position = owner * most + jnp.sum(before.astype(jnp.int32), axis=1)
    matched = jnp.logical_and(
        position[None, :] == jnp.arange(seats, dtype=jnp.int32)[:, None],
        slot_ids[None, :] < live_count,
    )
    filled = jnp.any(matched, axis=1)

    def seat_of(values):
        return jnp.sum(jnp.where(matched, values[None, :], 0), axis=1)

    seat_row = seat_of(row_block)
    seat_block = jnp.where(filled, seat_of(local_block), blocks)
    gathered = gather_rows(seat_block, row_count)
    arrived = lax.dynamic_slice_in_dim(
        gathered, lax.axis_index("row") * most, most, axis=1
    ).reshape(seats)
    in_runs = sorted_runs(arrived, blocks)
    row_runs = sorted_runs(seat_row, col_count * blocks)
    fields = {
        "slot": seat_of(slot_ids),
        "fill": -filled.astype(jnp.int32),
        "row": seat_row,
        "block": jnp.minimum(arrived, blocks - 1),
    }
    for prefix, runs in (("in", in_runs), ("row", row_runs)):
        for name, values in zip(("order", "same", "last", "some"), runs):
            fields[prefix + "_" + name] = values
    layout = {}
    used = 0
    for name, values in fields.items():
        layout[name] = used
        used += values.shape[0]
    table = jnp.concatenate(list(fields.values()))

    vmem = pl.BlockSpec(memory_space=pltpu.VMEM)
    half_shape = (row_all // 2, tile_size)
    dma = pltpu.SemaphoreType.DMA

    def chains(count, dtype):
        return tuple(pltpu.VMEM((count,) + half_shape, dtype) for _ in range(4))

    scratch = [
        chains(col_count * blocks, jnp.bfloat16),
        chains(seats, jnp.int16),
        chains(seats, jnp.int16),
        chains(seats, jnp.bfloat16),
        chains(seats, jnp.bfloat16),
        chains(blocks, jnp.bfloat16),
        chains(blocks, jnp.float32),
        chains(blocks, jnp.float32),
        pltpu.VMEM((2, blocks) + half_shape, jnp.float32),
        pltpu.VMEM((2, blocks) + half_shape, jnp.float32),
        pltpu.VMEM((seats,) + half_shape, jnp.float32),
        pltpu.VMEM((seats,) + half_shape, jnp.float32),
        dma((4, row_count)),
        dma((4, row_count)),
        dma((4, row_count)),
        dma((4, row_count)),
        dma((4,)),
        dma((4,)),
        dma((4,)),
        dma((4,)),
    ]
    dependency, centrality = pl.pallas_call(
        functools.partial(kernel, layout, row_count, col_count, most, blocks),
        out_shape=(
            jax.ShapeDtypeStruct((row_all, width), jnp.float32),
            jax.ShapeDtypeStruct((1, width), jnp.float32),
        ),
        in_specs=[pl.BlockSpec(memory_space=pltpu.SMEM), vmem, vmem, vmem, vmem],
        out_specs=(vmem, vmem),
        scratch_shapes=scratch,
        compiler_params=pltpu.CompilerParams(
            collective_id=0, has_side_effects=True, vmem_limit_bytes=60 * 1024 * 1024
        ),
        cost_estimate=pl.CostEstimate(
            flops=8 * seats * row_all * tile_size * tile_size,
            bytes_accessed=4 * tile_bits.size + 16 * row_all * width,
            transcendentals=4 * seats * row_all * tile_size,
        ),
    )(
        table,
        tile_bits.reshape(slot_total, tile_size // 8, tile_size),
        first_counts.reshape(row_all, width),
        depth.reshape(row_all, width),
        sources.reshape(row_all, 1),
    )
    return dependency.reshape(batch_count, src_count, width), centrality.reshape(width)


def solution(mesh):
    placed = (
        P("groups", None, ("row", "col")),
        P("groups", None, ("row", "col")),
        P("groups", None),
        P(("groups", "row"), "col", None),
        P(("groups", "row"), "col"),
        P(("groups", "row"), "col", None, None, None),
    )
    return jax.shard_map(
        shards,
        mesh=mesh,
        in_specs=placed,
        out_specs=(P("groups", None, ("row", "col")), P(("groups", "row", "col"))),
        check_vma=False,
    )
```

```python
import functools

import jax
import jax.numpy as jnp
from jax import lax
from jax.experimental import pallas as pl
from jax.experimental.pallas import tpu as pltpu
from jax.sharding import PartitionSpec as P

DEPTH = 8
STEPS = 2000.0
CODE_ZERO = -32768
MESH = pl.DeviceIdType.MESH


def encode(values):
    code = (jnp.log2(jnp.maximum(values, 1.0)) * STEPS + 0.5).astype(jnp.int32) + (CODE_ZERO + 1)
    return jnp.where(values > 0.0, code, CODE_ZERO).astype(jnp.int16)


def decode(code):
    wide = code.astype(jnp.int32)
    value = jnp.exp2((wide - (CODE_ZERO + 1)).astype(jnp.float32) * (1.0 / STEPS))
    return jnp.where(wide > CODE_ZERO, value, 0.0)


def unpack(words):
    count, width = words.shape
    shifts = lax.broadcasted_iota(jnp.int32, (count, 8, width), 1)
    bits = jnp.bitwise_and(jnp.right_shift(words[:, None, :], shifts), 1)
    return bits.reshape(count * 8, width).astype(jnp.float32).astype(jnp.bfloat16)


def loop(count, body):
    def step(index, carry):
        body(index)
        return carry

    lax.fori_loop(0, count, step, 0)


def divisor(count, most):
    return max(part for part in range(1, most + 1) if count % part == 0)


def grouped(count, size, compute, store):
    def body(group):
        indices = [group * size + place for place in range(size)]
        values = [compute(index) for index in indices]
        for index, value in zip(indices, values):
            store(index, value)

    if count == size:
        body(0)
    else:
        loop(count // size, body)


def gather_kernel(rows, mine, result, landed, sent, got):
    row = lax.axis_index("row")
    barrier = pltpu.get_barrier_semaphore()

    def greet(step):
        peer = lax.rem(row + step + 1, rows)
        pl.semaphore_signal(barrier, inc=1, device_id={"row": peer}, device_id_type=MESH)

    loop(rows - 1, greet)
    pl.semaphore_wait(barrier, rows - 1)

    def copy(source, target):
        return pltpu.make_async_remote_copy(
            src_ref=mine,
            dst_ref=landed.at[source],
            send_sem=sent.at[target],
            recv_sem=got.at[source],
            device_id={"row": target},
            device_id_type=MESH,
        )

    loop(rows - 1, lambda step: copy(row, lax.rem(row + step + 1, rows)).start())
    landed[row] = mine[...]

    def arrive(step):
        peer = lax.rem(row + step + 1, rows)
        copy(peer, peer).wait_recv()

    loop(rows - 1, arrive)
    result[...] = landed[...]
    loop(rows - 1, lambda step: copy(row, lax.rem(row + step + 1, rows)).wait_send())


def gather_rows(values, rows):
    lanes = (values.shape[0] + 127) // 128 * 128
    padded = jnp.broadcast_to(jnp.pad(values, (0, lanes - values.shape[0]))[None, :], (8, lanes))
    vmem = pl.BlockSpec(memory_space=pltpu.VMEM)
    gathered = pl.pallas_call(
        functools.partial(gather_kernel, rows),
        out_shape=jax.ShapeDtypeStruct((rows, 8, lanes), values.dtype),
        in_specs=[vmem],
        out_specs=vmem,
        scratch_shapes=[
            pltpu.VMEM((rows, 8, lanes), values.dtype),
            pltpu.SemaphoreType.DMA((rows,)),
            pltpu.SemaphoreType.DMA((rows,)),
        ],
        compiler_params=pltpu.CompilerParams(collective_id=1, has_side_effects=True),
    )(padded)
    return gathered[:, 0, :]


def kernel(
    layout,
    rows,
    cols,
    most,
    blocks,
    table,
    words,
    first,
    depth,
    sources,
    dependency,
    centrality,
    stripe,
    code_out,
    code_in,
    weight_out,
    weight_in,
    weights,
    sum_out,
    sum_in,
    counts1,
    delta1,
    running,
    terms,
    code_sent,
    code_got,
    weight_sent,
    weight_got,
    stripe_sent,
    stripe_got,
    sum_sent,
    sum_got,
):
    seats = rows * most
    tile = words.shape[-1]
    half_rows = running.shape[1]
    several = divisor(most, 2)
    some_blocks = divisor(blocks, 4)
    row = lax.axis_index("row")
    col = lax.axis_index("col")
    partner = 1 - col

    def entry(name, index):
        return table[layout[name] + index]

    barrier = pltpu.get_barrier_semaphore()

    def distance(step):
        return 1 + lax.rem(step + rows // 2 - 1, rows - 1)

    def leaving(step):
        return lax.rem(row + distance(step), rows)

    def arriving(step):
        return lax.rem(row + rows - distance(step), rows)

    def greet(step):
        pl.semaphore_signal(barrier, inc=1, device_id={"row": leaving(step)}, device_id_type=MESH)

    loop(rows - 1, greet)
    pl.semaphore_signal(barrier, inc=1, device_id={"col": partner}, device_id_type=MESH)

    def lanes(block):
        return pl.ds(pl.multiple_of(block * tile, tile), tile)

    def view(ref, half, block):
        return ref[half * half_rows : (half + 1) * half_rows, lanes(block)]

    def tile_of(seat):
        return unpack(jnp.bitwise_and(words[entry("slot", seat)], entry("fill", seat)))

    def stripe_copy(chain, owner):
        part = pl.ds(owner * blocks, blocks)
        return pltpu.make_async_remote_copy(
            src_ref=stripe[chain].at[part],
            dst_ref=stripe[chain].at[part],
            send_sem=stripe_sent.at[chain],
            recv_sem=stripe_got.at[chain],
            device_id={"col": partner},
            device_id_type=MESH,
        )

    def seat_copy(out, into, sent, got, chain, src_row, dst_row, peer):
        return pltpu.make_async_remote_copy(
            src_ref=out[chain].at[pl.ds(dst_row * most, most)],
            dst_ref=into[chain].at[pl.ds(src_row * most, most)],
            send_sem=sent.at[chain, dst_row],
            recv_sem=got.at[chain, src_row],
            device_id={"row": peer},
            device_id_type=MESH,
        )

    def code_copy(chain, src_row, dst_row, peer):
        return seat_copy(code_out, code_in, code_sent, code_got, chain, src_row, dst_row, peer)

    def weight_copy(chain, src_row, dst_row, peer):
        return seat_copy(
            weight_out, weight_in, weight_sent, weight_got, chain, src_row, dst_row, peer
        )

    def sum_copy(chain):
        return pltpu.make_async_remote_copy(
            src_ref=sum_out[chain],
            dst_ref=sum_in[chain],
            send_sem=sum_sent.at[chain],
            recv_sem=sum_got.at[chain],
            device_id={"col": partner},
            device_id_type=MESH,
        )

    def segment_sums(load, order, same):
        size = divisor(seats, 8)

        def group(number, total):
            indices = [number * size + place for place in range(size)]
            loaded = [load(entry(order, index)) for index in indices]
            totals = []
            for index, value in zip(indices, loaded):
                total = total * entry(same, index).astype(jnp.float32) + value
                totals.append(total)
            for index, value in zip(indices, totals):
                running[index] = value
            return total

        lax.fori_loop(0, seats // size, group, jnp.zeros(running.shape[1:], jnp.float32))

    def segment(last, some, block):
        return running[entry(last, block)] * entry(some, block).astype(jnp.float32)

    def forward_send(chain):
        stripe_copy(chain, partner).wait_recv()

        def product(seat):
            piece = stripe[chain][entry("row", seat)]
            return encode(jnp.dot(piece, tile_of(seat), preferred_element_type=jnp.float32))

        def send(step):
            peer = leaving(step)

            def keep(place, value):
                code_out[chain][peer * most + place] = value

            grouped(most, several, lambda place: product(peer * most + place), keep)
            code_copy(chain, row, peer, peer).start()

        loop(rows - 1, send)

        def own(place, value):
            code_in[chain][row * most + place] = value

        grouped(most, several, lambda place: product(row * most + place), own)

    def forward_sum(chain, finish):
        def arrive(step):
            peer = arriving(step)
            code_copy(chain, peer, row, peer).wait_recv()

        loop(rows - 1, arrive)
        segment_sums(lambda seat: decode(code_in[chain][seat]), "in_order", "in_same")
        grouped(blocks, some_blocks, lambda block: segment("in_last", "in_some", block), finish)

    def backward_send(chain):
        def owned(seat):
            return weights[chain][entry("block", seat)]

        def send(step):
            peer = leaving(step)

            def keep(place, value):
                weight_out[chain][peer * most + place] = value

            grouped(most, several, lambda place: owned(peer * most + place), keep)
            weight_copy(chain, row, peer, peer).start()

        loop(rows - 1, send)

    def backward_sum(chain, finish):
        def product(seat, piece):
            return lax.dot_general(
                piece, tile_of(seat), (((1,), (1,)), ((), ())), preferred_element_type=jnp.float32
            )

        def products(peer, piece):
            def keep(place, value):
                terms[peer * most + place] = value

            def one(place):
                return product(peer * most + place, piece(peer * most + place))

            grouped(most, several, one, keep)

        products(row, lambda seat: weights[chain][entry("block", seat)])

        def arrive(step):
            peer = arriving(step)
            weight_copy(chain, peer, row, peer).wait_recv()
            products(peer, lambda seat: weight_in[chain][seat])

        loop(rows - 1, arrive)
        segment_sums(lambda seat: terms[seat], "row_order", "row_same")

        def leaves(block):
            return segment("row_last", "row_some", partner * blocks + block)

        def leave(block, value):
            sum_out[chain][block] = value

        grouped(blocks, some_blocks, leaves, leave)
        sum_copy(chain).start()
        sum_copy(chain).wait_recv()

        def total(block):
            mine = segment("row_last", "row_some", col * blocks + block)
            return mine + sum_in[chain][block]

        grouped(blocks, some_blocks, total, finish)

    def start(half):
        def masked(block):
            counts0 = view(first, half, block).astype(jnp.float32)
            values = jnp.where(view(depth, half, block) == DEPTH - 2, counts0, 0.0)
            return values.astype(jnp.bfloat16)

        def keep(block, value):
            stripe[half][col * blocks + block] = value

        grouped(blocks, some_blocks, masked, keep)

    def middle_counts(half, block, total):
        counts = jnp.where(view(depth, half, block) == DEPTH - 1, total, 0.0)
        counts1[half, block] = counts
        stripe[2 + half][col * blocks + block] = counts.astype(jnp.bfloat16)

    def last_weights(half, block, total):
        last = view(depth, half, block) == DEPTH
        weight = jnp.where(last, 1.0 / jnp.maximum(total, 1.0), 0.0)
        weights[half][block] = weight.astype(jnp.bfloat16)

    def middle_weights(half, block, total):
        middle = view(depth, half, block) == DEPTH - 1
        counts = counts1[half, block]
        delta = jnp.where(middle, counts * total, 0.0)
        delta1[half, block] = delta
        weight = jnp.where(middle, (1.0 + delta) / jnp.maximum(counts, 1.0), 0.0)
        weights[2 + half][block] = weight.astype(jnp.bfloat16)

    offset = (row * cols + col) * (blocks * tile)

    def results(half, block, total):
        counts0 = view(first, half, block).astype(jnp.float32)
        delta = jnp.where(view(depth, half, block) == DEPTH - 2, counts0 * total, 0.0)
        value = delta1[half, block] + delta
        mine = slice(half * half_rows, (half + 1) * half_rows)
        dependency[mine, lanes(block)] = value
        vertex = lax.broadcasted_iota(jnp.int32, value.shape, 1) + (offset + block * tile)
        kept = jnp.where(vertex != sources[mine, :], value, 0.0)
        part = jnp.sum(kept, axis=0, keepdims=True)
        if half == 0:
            centrality[:, lanes(block)] = part
        else:
            centrality[:, lanes(block)] = centrality[:, lanes(block)] + part

    halves = (0, 1)
    for half in halves:
        start(half)
        if half == 0:
            pl.semaphore_wait(barrier, rows)
        stripe_copy(half, col).start()
    for half in halves:
        forward_send(half)
    for half in halves:
        forward_sum(half, functools.partial(middle_counts, half))
        stripe_copy(2 + half, col).start()
        forward_send(2 + half)
    for half in halves:
        forward_sum(2 + half, functools.partial(last_weights, half))
        backward_send(half)
    for half in halves:
        backward_sum(half, functools.partial(middle_weights, half))
        backward_send(2 + half)
    for half in halves:
        backward_sum(2 + half, functools.partial(results, half))

    for chain in range(4):
        stripe_copy(chain, col).wait_send()
        sum_copy(chain).wait_send()

        def sent(step, chain=chain):
            peer = leaving(step)
            code_copy(chain, row, peer, peer).wait_send()
            weight_copy(chain, row, peer, peer).wait_send()

        loop(rows - 1, sent)


def sorted_runs(keys, kinds):
    seats = keys.shape[0]
    ids = jnp.arange(seats, dtype=jnp.int32)
    ahead = jnp.logical_or(
        keys[None, :] < keys[:, None],
        jnp.logical_and(keys[None, :] == keys[:, None], ids[None, :] < ids[:, None]),
    )
    rank = jnp.sum(ahead.astype(jnp.int32), axis=1)
    placed = rank[None, :] == ids[:, None]
    order = jnp.sum(jnp.where(placed, ids[None, :], 0), axis=1)
    equal_before = jnp.logical_and(keys[None, :] == keys[:, None], ids[None, :] < ids[:, None])
    repeated = jnp.any(equal_before, axis=1)
    same = jnp.sum(jnp.where(placed, repeated[None, :], False).astype(jnp.int32), axis=1)
    kind_ids = jnp.arange(kinds, dtype=jnp.int32)
    upto = jnp.sum((keys[None, :] <= kind_ids[:, None]).astype(jnp.int32), axis=1)
    last = jnp.maximum(upto - 1, 0)
    some = jnp.any(keys[None, :] == kind_ids[:, None], axis=1).astype(jnp.int32)
    return order, same, last, some


def shards(first_counts, depth, sources, tile_pos, tile_live, tile_bits):
    batch_count, src_count, width = first_counts.shape
    row_count = lax.axis_size("row")
    col_count = lax.axis_size("col")
    tile_size = tile_bits.shape[-1]
    slot_total = tile_bits.shape[2]
    row_all = batch_count * src_count
    blocks = width // tile_size
    most = (slot_total + row_count - 1) // row_count
    seats = row_count * most
    live_count = tile_live.reshape(())
    places = tile_pos.reshape(slot_total)
    stripe_span = row_count * blocks
    row_block = places // stripe_span
    column = places % stripe_span
    owner = column // blocks
    local_block = column % blocks
    slot_ids = jnp.arange(slot_total, dtype=jnp.int32)
    before = jnp.logical_and(
        owner[:, None] == owner[None, :], slot_ids[None, :] < slot_ids[:, None]
    )
    position = owner * most + jnp.sum(before.astype(jnp.int32), axis=1)
    matched = jnp.logical_and(
        position[None, :] == jnp.arange(seats, dtype=jnp.int32)[:, None],
        slot_ids[None, :] < live_count,
    )
    filled = jnp.any(matched, axis=1)

    def seat_of(values):
        return jnp.sum(jnp.where(matched, values[None, :], 0), axis=1)

    seat_row = seat_of(row_block)
    seat_block = jnp.where(filled, seat_of(local_block), blocks)
    gathered = gather_rows(seat_block, row_count)
    arrived = lax.dynamic_slice_in_dim(
        gathered, lax.axis_index("row") * most, most, axis=1
    ).reshape(seats)
    in_runs = sorted_runs(arrived, blocks)
    row_runs = sorted_runs(seat_row, col_count * blocks)
    fields = {
        "slot": seat_of(slot_ids),
        "fill": -filled.astype(jnp.int32),
        "row": seat_row,
        "block": jnp.minimum(arrived, blocks - 1),
    }
    for prefix, runs in (("in", in_runs), ("row", row_runs)):
        for name, values in zip(("order", "same", "last", "some"), runs):
            fields[prefix + "_" + name] = values
    layout = {}
    used = 0
    for name, values in fields.items():
        layout[name] = used
        used += values.shape[0]
    table = jnp.concatenate(list(fields.values()))

    vmem = pl.BlockSpec(memory_space=pltpu.VMEM)
    half_shape = (row_all // 2, tile_size)
    dma = pltpu.SemaphoreType.DMA

    def chains(count, dtype):
        return tuple(pltpu.VMEM((count,) + half_shape, dtype) for _ in range(4))

    scratch = [
        chains(col_count * blocks, jnp.bfloat16),
        chains(seats, jnp.int16),
        chains(seats, jnp.int16),
        chains(seats, jnp.bfloat16),
        chains(seats, jnp.bfloat16),
        chains(blocks, jnp.bfloat16),
        chains(blocks, jnp.float32),
        chains(blocks, jnp.float32),
        pltpu.VMEM((2, blocks) + half_shape, jnp.float32),
        pltpu.VMEM((2, blocks) + half_shape, jnp.float32),
        pltpu.VMEM((seats,) + half_shape, jnp.float32),
        pltpu.VMEM((seats,) + half_shape, jnp.float32),
        dma((4, row_count)),
        dma((4, row_count)),
        dma((4, row_count)),
        dma((4, row_count)),
        dma((4,)),
        dma((4,)),
        dma((4,)),
        dma((4,)),
    ]
    dependency, centrality = pl.pallas_call(
        functools.partial(kernel, layout, row_count, col_count, most, blocks),
        out_shape=(
            jax.ShapeDtypeStruct((row_all, width), jnp.float32),
            jax.ShapeDtypeStruct((1, width), jnp.float32),
        ),
        in_specs=[pl.BlockSpec(memory_space=pltpu.SMEM), vmem, vmem, vmem, vmem],
        out_specs=(vmem, vmem),
        scratch_shapes=scratch,
        compiler_params=pltpu.CompilerParams(
            collective_id=0, has_side_effects=True, vmem_limit_bytes=60 * 1024 * 1024
        ),
        cost_estimate=pl.CostEstimate(
            flops=8 * seats * row_all * tile_size * tile_size,
            bytes_accessed=4 * tile_bits.size + 16 * row_all * width,
            transcendentals=4 * seats * row_all * tile_size,
        ),
    )(
        table,
        tile_bits.reshape(slot_total, tile_size // 8, tile_size),
        first_counts.reshape(row_all, width),
        depth.reshape(row_all, width),
        sources.reshape(row_all, 1),
    )
    return dependency.reshape(batch_count, src_count, width), centrality.reshape(width)


def solution(mesh):
    placed = (
        P("groups", None, ("row", "col")),
        P("groups", None, ("row", "col")),
        P("groups", None),
        P(("groups", "row"), "col", None),
        P(("groups", "row"), "col"),
        P(("groups", "row"), "col", None, None, None),
    )
    return jax.shard_map(
        shards,
        mesh=mesh,
        in_specs=placed,
        out_specs=(P("groups", None, ("row", "col")), P(("groups", "row", "col"))),
        check_vma=False,
    )
```
